32 devices in a mesh: shot: 2 (over y), depth: 2 (over core), lat: 8 (over z, x).
Axes of the slice: x: 2, y: 2, z: 4, core: 2. Of those that a mesh axis runs over, the one named last changes fastest.
Arguments:
- sources: float32 [6, 2, 32, 4096], P('shot', None, 'depth', 'lat'), parts along dimension 0, may hold values from -6 to 6
- blocks: float32 [4, 32, 7, 2, 128, 128], P(('shot', 'depth'), 'lat'), parts along dimension 0, may hold values from -0.125 to 0.125
- block_cols: int32 [2, 32, 7], P('depth', 'lat'), may hold values from 0 to 31, as said below
- refl_level: int32 [4096], P('lat'), may hold values from 0 to 1
- refl_coef: float32 [2, 4096], P(None, 'lat'), may hold values from -0.5 to 0.5
Outputs:
- bottom: float32 [6, 2, 32, 4096], P('shot', None, 'depth', 'lat'), parts along dimension 0
The draws below stay inside these ranges and needn't reach their ends.
There are 2 independent parts, one for each index of `shot`. The reference program is written for one: setup_inputs(seed, part) draws one part's arguments, and reference() takes and returns one part's arrays. A program takes and returns all parts, laid end to end along the dimension named above; an argument that names none is the same for every part. Nothing has to cross between parts.
Inputs may be any that keep to these rules, and one draw needn't show every extreme that they name: block_cols[l, b, 0] = b, and every entry of row b lies within 4 block rows of b; a row may name a column twice.
All inputs are finite; a program needn't handle non-finite values.
Results may differ from the reference program's by a relative error of at most 0.0001.
Values sent between devices are 32-bit elements; how exact they have to be, the bound alone decides.
A program may use at most 64 MiB of HBM per device.

```python
import jax
import jax.numpy as jnp
from jax import lax

B = 128
NNZ = 7
PANELS = 3
S = 32
BR_DEV = 4
LEVELS = 2
NB = 32
NPTS = 4096


def draw_block_cols(key, part):
    reach_rows = BR_DEV
    candidates = jnp.concatenate([jnp.arange(-reach_rows, 0), jnp.arange(1, reach_rows + 1)]).astype(jnp.int32)
    scores = jax.random.randint(key, (LEVELS, NB, 2 * reach_rows), 0, 1 << 20).astype(jnp.int32)
    scores = scores * (2 * reach_rows) + jnp.arange(2 * reach_rows).astype(jnp.int32)
    chosen = jnp.argsort(scores, axis=-1)[:, :, :NNZ - 1]
    offsets = candidates[chosen]
    row_ids = jnp.arange(NB).astype(jnp.int32)[None, :, None]
    columns = row_ids + offsets
    columns = jnp.where((columns < 0) | (columns >= NB), row_ids - offsets, columns)
    diagonal = jnp.broadcast_to(row_ids, (LEVELS, NB, 1))
    return jnp.concatenate([diagonal, columns], axis=-1).astype(jnp.int32)


def set_ends(result, stream_key, low, largest):
    place = [jax.random.randint(jax.random.fold_in(stream_key, axis), (), 0, length) for axis, length in enumerate(result.shape)]
    longest = result.shape.index(max(result.shape))
    beside = place[:longest] + [(place[longest] + 1) % result.shape[longest]] + place[longest + 1:]
    return result.at[tuple(place)].set(low).at[tuple(beside)].set(largest)


def level_of(stream_key, shape, shards, least, largest):
    gain = 1.0
    for axis_at, shards_of in shards:
        heights = jax.random.uniform(jax.random.fold_in(jax.random.fold_in(stream_key, 6), axis_at), (shards_of,), jnp.float32, least / len(shards), largest / len(shards))
        gain = gain * jnp.repeat(jnp.exp(heights), shape[axis_at] // shards_of).reshape((-1,) + (1,) * (len(shape) - 1 - axis_at))
    return gain


def gaussian(stream_key, dims, width, limit, split=(), dtype=jnp.bfloat16):
    gain = level_of(stream_key, dims, split, -0.22, 0.18) if split else 1.0
    drawn = jax.random.normal(stream_key, dims, jnp.float32) * width * gain
    return jnp.minimum(jnp.maximum(drawn, -limit), limit).astype(dtype)


def setup_inputs(seed: int = 0, part: int = 0) -> dict:
    arg_keys = jax.random.split(jax.random.key(seed), 6)
    own_keys = jax.random.split(jax.random.fold_in(arg_keys[5], part), 6)
    sources = gaussian(own_keys[0], (PANELS, 2, S, NPTS), 1.0, 6.0, ((2, 2), (3, 8)), jnp.float32)
    blocks = gaussian(own_keys[1], (LEVELS, NB, NNZ, 2, B, B), (2 * NNZ * B) ** -0.5, 0.125, ((0, 2), (1, 8)), jnp.float32)
    block_cols = draw_block_cols(jax.random.fold_in(arg_keys[5], 71), part)
    refl_level = set_ends(jax.random.randint(arg_keys[3], (NPTS,), 0, LEVELS), jax.random.fold_in(arg_keys[3], 1), 0, LEVELS - 1).astype(jnp.int32)
    refl_coef = jnp.clip(jax.random.uniform(arg_keys[4], (2, NPTS), jnp.float32, -0.5, 0.5) * level_of(arg_keys[4], (2, NPTS), ((1, 8),), -0.4, 0.0), -0.5, 0.5)
    return {"sources": sources, "blocks": blocks, "block_cols": block_cols, "refl_level": refl_level, "refl_coef": refl_coef}


def reference(sources, blocks, block_cols, refl_level, refl_coef):
    channels = PANELS * S
    wavefield = jnp.transpose(sources, (1, 0, 2, 3)).reshape(2, channels, NPTS)
    for level_index in range(LEVELS):
        at_level = refl_level == level_index
        coef_re = jnp.where(at_level, refl_coef[0], jnp.float32(0.0))
        coef_im = jnp.where(at_level, refl_coef[1], jnp.float32(0.0))
        field_re = wavefield[0]
        field_im = wavefield[1]
        combined = jnp.concatenate([field_re + coef_re * field_re - coef_im * field_im,
                                    field_im + coef_re * field_im + coef_im * field_re], axis=0)
        stacked = combined.reshape(2 * channels, NB, B)

        def one_row(row_args):
            row_cols, row_blocks = row_args
            picked = jnp.take(stacked, row_cols, axis=1)
            real_part = jnp.einsum("cjp,jpq->cq", picked, row_blocks[:, 0], precision=lax.Precision.HIGHEST)
            imag_part = jnp.einsum("cjp,jpq->cq", picked, row_blocks[:, 1], precision=lax.Precision.HIGHEST)
            return jnp.concatenate([real_part[:channels] - imag_part[channels:],
                                    imag_part[:channels] + real_part[channels:]], axis=0)

        rows_out = lax.map(one_row, (block_cols[level_index], blocks[level_index]))
        wavefield = jnp.transpose(rows_out, (1, 0, 2)).reshape(2, channels, NPTS)
    return jnp.transpose(wavefield.reshape(2, PANELS, S, NPTS), (1, 0, 2, 3))
```

```python
import functools

import jax
import jax.numpy as jnp
from jax import lax
from jax.experimental import pallas as pl
from jax.experimental.pallas import tpu as pltpu
from jax.sharding import PartitionSpec as P

MESH = pl.DeviceIdType.MESH


def split_bf16(value):
    high = value.astype(jnp.bfloat16)
    low = (value - high.astype(jnp.float32)).astype(jnp.bfloat16)
    return high, low


def kernel(
    lat_count, blocks, cols, sources, level, coef, out,
    raw, w_hi, w_lo, src, lev, cf, entering, field, parts, stage, final,
    load_w, load_s, load_r,
    send_c, send_x, send_z, send_cx, send_cc, send_o,
    recv_c, recv_x, recv_z, recv_o, store_o,
):
    panels, _, part, points = sources.shape
    _, rows, per_row, _, size, _ = blocks.shape
    half = 2 * part
    depth = lax.axis_index("depth")
    lat = lax.axis_index("lat")
    odd = lax.rem(lat, 2)
    pair = lat + 1 - 2 * odd
    onward = lat + 2 - 4 * odd
    behind = lat - 2 + 4 * odd
    has_onward = jnp.logical_and(onward >= 0, onward < lat_count)
    has_behind = jnp.logical_and(behind >= 0, behind < lat_count)
    near = 2 * rows * (1 - odd)
    far = 2 * rows * odd

    weight_loads = [
        pltpu.make_async_copy(blocks.at[0, b], raw.at[b], load_w.at[b]) for b in range(rows)
    ]
    source_loads = [
        pltpu.make_async_copy(sources.at[k], src.at[k], load_s.at[k]) for k in range(panels)
    ]
    refl_loads = [
        pltpu.make_async_copy(level, lev, load_r.at[0]),
        pltpu.make_async_copy(coef, cf, load_r.at[1]),
    ]
    for copy in refl_loads + source_loads + weight_loads:
        copy.start()

    barrier = pltpu.get_barrier_semaphore()
    pl.semaphore_signal(barrier, device_id={"depth": 1 - depth, "lat": lat}, device_id_type=MESH)
    pl.semaphore_signal(barrier, device_id={"depth": 1 - depth, "lat": pair}, device_id_type=MESH)

    @pl.when(depth == 0)
    def _():
        pl.semaphore_signal(barrier, device_id={"depth": 0, "lat": pair}, device_id_type=MESH)

    @pl.when(has_behind)
    def _():
        pl.semaphore_signal(barrier, device_id={"depth": depth, "lat": behind}, device_id_type=MESH)

    for copy in refl_loads:
        copy.wait()

    def coefficients(at):
        here = lev[...] == at
        zero = jnp.float32(0.0)
        return jnp.where(here, cf[0:1, :], zero), jnp.where(here, cf[1:2, :], zero)

    def reflected(re, im, c_re, c_im):
        return re + c_re * re - c_im * im, im + c_re * im + c_im * re

    def send(src_ref, dst_ref, send_sem, recv_sem, to_depth, to_lat):
        return pltpu.make_async_remote_copy(
            src_ref=src_ref, dst_ref=dst_ref, send_sem=send_sem, recv_sem=recv_sem,
            device_id={"depth": to_depth, "lat": to_lat}, device_id_type=MESH,
        )

    def entering_across(k):
        return send(
            entering.at[k], field.at[k, depth, pl.ds(far, rows)],
            send_x.at[k], recv_x.at[k, depth], 0, pair,
        )

    def entering_own(k):
        return send(
            entering.at[k], field.at[k, 1, pl.ds(rows, rows)],
            send_c.at[k], recv_c.at[k, 1], 0, lat,
        )

    def leaving_across(k, d):
        return send(
            stage.at[k, d], field.at[k, d, pl.ds(far, rows)],
            send_cx.at[k, d], recv_x.at[k, d], 1, pair,
        )

    def leaving_own(k, d):
        return send(
            stage.at[k, d], field.at[k, d, pl.ds(rows, rows)],
            send_cc.at[k, d], recv_c.at[k, d], 1, lat,
        )

    def onward_copy(k, d):
        return send(
            field.at[k, d, pl.ds(near, rows)], field.at[k, d, pl.ds(far, rows)],
            send_z.at[k, d], recv_z.at[k, d], depth, onward,
        )

    def return_copy(k):
        return send(final.at[k, 0], out.at[k], send_o.at[k], recv_o.at[k], 0, lat)

    c_re, c_im = coefficients(0)
    for k in range(panels):
        source_loads[k].wait()
        for b in range(rows):
            at = slice(b * size, (b + 1) * size)
            re, im = reflected(src[k, 0, :, at], src[k, 1, :, at], c_re[:, at], c_im[:, at])
            entering[k, b, 0:part] = re
            entering[k, b, part:half] = im

            @pl.when(depth == 0)
            def _():
                field[k, 0, rows + b, 0:part] = re
                field[k, 0, rows + b, part:half] = im

        if k == 0:
            pl.semaphore_wait(barrier, 3 - depth + has_onward.astype(jnp.int32))
        entering_across(k).start()

        @pl.when(depth == 1)
        def _():
            entering_own(k).start()

    for b in range(rows):
        weight_loads[b].wait()

        @pl.loop(0, per_row)
        def _(j):
            for c in range(2):
                high, low = split_bf16(raw[b, j, c])
                at = pl.ds(pl.multiple_of(j * size, size), size)
                w_hi[b, at, c * size:(c + 1) * size] = high
                w_lo[b, at, c * size:(c + 1) * size] = low

    def pass_on(k):
        for d in range(2):
            leaving_across(k, d).wait_recv()

            @pl.when(has_onward)
            def _():
                onward_copy(k, d).start()

    c_re, c_im = coefficients(1)
    base = (lat - 1) * rows
    pass_on(0)
    for k in range(panels):
        if k + 1 < panels:
            pass_on(k + 1)

        @pl.when(depth == 1)
        def _():
            leaving_own(k, 0).wait_recv()

        leaving_own(k, 1).wait_recv()

        @pl.when(has_behind)
        def _():
            for d in range(2):
                onward_copy(k, d).wait_recv()

        for slot in range(3 * rows):
            for d in range(2):
                high, low = split_bf16(field[k, d, slot])
                parts[k, slot, d * half:(d + 1) * half] = high
                parts[k, slot, (2 + d) * half:(3 + d) * half] = low

        for b in range(rows):
            picked = jnp.concatenate(
                [parts[k, jnp.clip(cols[0, b, j] - base, 0, 3 * rows - 1)] for j in range(per_row)],
                axis=1,
            )
            both = jnp.dot(picked, w_hi[b], preferred_element_type=jnp.float32)
            rest = jnp.dot(picked[:2 * half], w_lo[b], preferred_element_type=jnp.float32)
            total = both[:2 * half] + (both[2 * half:] + rest)
            at = slice(b * size, (b + 1) * size)
            leaving = []
            for d in range(2):
                of_re = total[d * half:d * half + part]
                of_im = total[d * half + part:(d + 1) * half]
                leaving.append(
                    (of_re[:, :size] - of_im[:, size:], of_re[:, size:] + of_im[:, :size])
                )

            @pl.when(depth == 0)
            def _():
                for d in range(2):
                    re, im = reflected(*leaving[d], c_re[:, at], c_im[:, at])
                    stage[k, d, b, 0:part] = re
                    stage[k, d, b, part:half] = im

            @pl.when(depth == 1)
            def _():
                for d in range(2):
                    for c in range(2):
                        final[k, d, c, :, at] = leaving[d][c]

        @pl.when(depth == 0)
        def _():
            for d in range(2):
                leaving_across(k, d).start()
            for d in range(2):
                leaving_own(k, d).start()

        @pl.when(depth == 1)
        def _():
            return_copy(k).start()
            pltpu.make_async_copy(final.at[k, 1], out.at[k], store_o.at[k]).start()

    @pl.when(depth == 0)
    def _():
        for k in range(panels):
            for d in range(2):
                leaving_across(k, d).wait_send()
                leaving_own(k, d).wait_send()
            return_copy(k).wait_recv()

    @pl.when(depth == 1)
    def _():
        for k in range(panels):
            entering_own(k).wait_send()
            return_copy(k).wait_send()
            pltpu.make_async_copy(final.at[k, 1], out.at[k], store_o.at[k]).wait()

    for k in range(panels):
        entering_across(k).wait_send()

    @pl.when(has_onward)
    def _():
        for k in range(panels):
            for d in range(2):
                onward_copy(k, d).wait_send()


def per_device(sources, blocks, block_cols, refl_level, refl_coef):
    lat_count = lax.axis_size("lat")
    assert lax.axis_size("depth") == 2 and blocks.shape[0] == 1 and lat_count % 2 == 0
    panels, _, part, points = sources.shape
    _, rows, per_row, _, size, _ = blocks.shape
    half = 2 * part
    f32, bf16 = jnp.float32, jnp.bfloat16
    dma = pltpu.SemaphoreType.DMA
    anywhere = pl.BlockSpec(memory_space=pl.ANY)
    flops = 2 * 3 * 4 * panels * part * 2 * rows * per_row * size * size * 2
    return pl.pallas_call(
        functools.partial(kernel, lat_count),
        out_shape=jax.ShapeDtypeStruct(sources.shape, f32),
        in_specs=[
            anywhere,
            pl.BlockSpec(memory_space=pltpu.SMEM),
            anywhere,
            anywhere,
            anywhere,
        ],
        out_specs=anywhere,
        scratch_shapes=[
            pltpu.VMEM((rows, per_row, 2, size, size), f32),
            pltpu.VMEM((rows, per_row * size, 2 * size), bf16),
            pltpu.VMEM((rows, per_row * size, 2 * size), bf16),
            pltpu.VMEM((panels, 2, part, points), f32),
            pltpu.VMEM((1, points), jnp.int32),
            pltpu.VMEM((2, points), f32),
            pltpu.VMEM((panels, rows, half, size), f32),
            pltpu.VMEM((panels, 2, 3 * rows, half, size), f32),
            pltpu.VMEM((panels, 3 * rows, 4 * half, size), bf16),
            pltpu.VMEM((panels, 2, rows, half, size), f32),
            pltpu.VMEM((panels, 2, 2, part, points), f32),
            dma((rows,)), dma((panels,)), dma((2,)),
            dma((panels,)), dma((panels,)), dma((panels, 2)),
            dma((panels, 2)), dma((panels, 2)), dma((panels,)),
            dma((panels, 2)), dma((panels, 2)), dma((panels, 2)),
            dma((panels,)), dma((panels,)),
        ],
        compiler_params=pltpu.CompilerParams(
            collective_id=0, has_side_effects=True, vmem_limit_bytes=63 * 1024 * 1024
        ),
        cost_estimate=pl.CostEstimate(
            flops=flops, bytes_accessed=4 * (blocks.size + 2 * sources.size), transcendentals=0
        ),
    )(blocks, block_cols, sources, refl_level.reshape(1, points), refl_coef)


def solution(mesh):
    placed = (
        P("shot", None, "depth", "lat"),
        P(("shot", "depth"), "lat", None, None, None, None),
        P("depth", "lat", None),
        P("lat"),
        P(None, "lat"),
    )
    return jax.shard_map(
        per_device,
        mesh=mesh,
        in_specs=placed,
        out_specs=P("shot", None, "depth", "lat"),
        check_vma=False,
    )
```

```python
import functools

import jax
import jax.numpy as jnp
from jax import lax
from jax.experimental import pallas as pl
from jax.experimental.pallas import tpu as pltpu
from jax.sharding import PartitionSpec as P

MESH = pl.DeviceIdType.MESH


def split_bf16(value):
    high = value.astype(jnp.bfloat16)
    low = (value - high.astype(jnp.float32)).astype(jnp.bfloat16)
    return high, low


def kernel(
    lat_count, blocks, cols, sources, level, coef, out,
    raw, w_hi, w_lo, src, lev, cf, entering, field, parts, stage, final,
    load_w, load_s, load_r,
    send_c, send_x, send_z, send_cx, send_cc, send_o,
    recv_c, recv_x, recv_z, recv_o, store_o,
):
    panels, _, part, points = sources.shape
    _, rows, per_row, _, size, _ = blocks.shape
    half = 2 * part
    depth = lax.axis_index("depth")
    lat = lax.axis_index("lat")
    odd = lax.rem(lat, 2)
    pair = lat + 1 - 2 * odd
    onward = lat + 2 - 4 * odd
    behind = lat - 2 + 4 * odd
    has_onward = jnp.logical_and(onward >= 0, onward < lat_count)
    has_behind = jnp.logical_and(behind >= 0, behind < lat_count)
    near = 2 * rows * (1 - odd)
    far = 2 * rows * odd

    weight_loads = [
        pltpu.make_async_copy(blocks.at[0, b], raw.at[b], load_w.at[b]) for b in range(rows)
    ]
    source_loads = [
        pltpu.make_async_copy(sources.at[k], src.at[k], load_s.at[k]) for k in range(panels)
    ]
    refl_loads = [
        pltpu.make_async_copy(level, lev, load_r.at[0]),
        pltpu.make_async_copy(coef, cf, load_r.at[1]),
    ]
    for copy in refl_loads + source_loads + weight_loads:
        copy.start()

    barrier = pltpu.get_barrier_semaphore()
    pl.semaphore_signal(barrier, device_id={"depth": 1 - depth, "lat": lat}, device_id_type=MESH)
    pl.semaphore_signal(barrier, device_id={"depth": 1 - depth, "lat": pair}, device_id_type=MESH)

    @pl.when(depth == 0)
    def _():
        pl.semaphore_signal(barrier, device_id={"depth": 0, "lat": pair}, device_id_type=MESH)

    @pl.when(has_behind)
    def _():
        pl.semaphore_signal(barrier, device_id={"depth": depth, "lat": behind}, device_id_type=MESH)

    for copy in refl_loads:
        copy.wait()

    def coefficients(at):
        here = lev[...] == at
        zero = jnp.float32(0.0)
        return jnp.where(here, cf[0:1, :], zero), jnp.where(here, cf[1:2, :], zero)

    def reflected(re, im, c_re, c_im):
        return re + c_re * re - c_im * im, im + c_re * im + c_im * re

    def send(src_ref, dst_ref, send_sem, recv_sem, to_depth, to_lat):
        return pltpu.make_async_remote_copy(
            src_ref=src_ref, dst_ref=dst_ref, send_sem=send_sem, recv_sem=recv_sem,
            device_id={"depth": to_depth, "lat": to_lat}, device_id_type=MESH,
        )

    def entering_across(k):
        return send(
            entering.at[k], field.at[k, depth, pl.ds(far, rows)],
            send_x.at[k], recv_x.at[k, depth], 0, pair,
        )

    def entering_own(k):
        return send(
            entering.at[k], field.at[k, 1, pl.ds(rows, rows)],
            send_c.at[k], recv_c.at[k, 1], 0, lat,
        )

    def leaving_across(k, d):
        return send(
            stage.at[k, d], field.at[k, d, pl.ds(far, rows)],
            send_cx.at[k, d], recv_x.at[k, d], 1, pair,
        )

    def leaving_own(k, d):
        return send(
            stage.at[k, d], field.at[k, d, pl.ds(rows, rows)],
            send_cc.at[k, d], recv_c.at[k, d], 1, lat,
        )

    def onward_copy(k, d):
        return send(
            field.at[k, d, pl.ds(near, rows)], field.at[k, d, pl.ds(far, rows)],
            send_z.at[k, d], recv_z.at[k, d], depth, onward,
        )

    def return_copy(k):
        return send(final.at[k, 0], out.at[k], send_o.at[k], recv_o.at[k], 0, lat)

    def send_entering(k):
        if k > 0:
            entering_across(k - 1).wait_send()
        entering_across(k).start()

        @pl.when(depth == 1)
        def _():
            entering_own(k).start()

    c_re, c_im = coefficients(0)
    for k in range(panels):
        source_loads[k].wait()
        for b in range(rows):
            at = slice(b * size, (b + 1) * size)
            re, im = reflected(src[k, 0, :, at], src[k, 1, :, at], c_re[:, at], c_im[:, at])
            entering[k, b, 0:part] = re
            entering[k, b, part:half] = im

            @pl.when(depth == 0)
            def _():
                field[k, 0, rows + b, 0:part] = re
                field[k, 0, rows + b, part:half] = im

        if k == 0:
            pl.semaphore_wait(barrier, 3 - depth + has_onward.astype(jnp.int32))
            send_entering(0)

    for b in range(rows):
        weight_loads[b].wait()

        @pl.loop(0, per_row)
        def _(j):
            for c in range(2):
                high, low = split_bf16(raw[b, j, c])
                at = pl.ds(pl.multiple_of(j * size, size), size)
                w_hi[b, at, c * size:(c + 1) * size] = high
                w_lo[b, at, c * size:(c + 1) * size] = low

    def pass_on(k):
        for d in range(2):
            leaving_across(k, d).wait_recv()

            @pl.when(has_onward)
            def _():
                onward_copy(k, d).start()

    c_re, c_im = coefficients(1)
    base = (lat - 1) * rows
    for k in range(panels):
        if k == 0 and panels > 1:
            send_entering(1)
            pass_on(0)
        if k + 2 < panels:
            send_entering(k + 2)
        if k + 1 < panels:
            pass_on(k + 1)
        if panels == 1:
            pass_on(0)

        @pl.when(depth == 1)
        def _():
            leaving_own(k, 0).wait_recv()

        leaving_own(k, 1).wait_recv()

        @pl.when(has_behind)
        def _():
            for d in range(2):
                onward_copy(k, d).wait_recv()

        for slot in range(3 * rows):
            for d in range(2):
                high, low = split_bf16(field[k, d, slot])
                parts[k, slot, d * half:(d + 1) * half] = high
                parts[k, slot, (2 + d) * half:(3 + d) * half] = low

        for b in range(rows):
            picked = jnp.concatenate(
                [parts[k, jnp.clip(cols[0, b, j] - base, 0, 3 * rows - 1)] for j in range(per_row)],
                axis=1,
            )
            both = jnp.dot(picked, w_hi[b], preferred_element_type=jnp.float32)
            rest = jnp.dot(picked[:2 * half], w_lo[b], preferred_element_type=jnp.float32)
            total = both[:2 * half] + (both[2 * half:] + rest)
            at = slice(b * size, (b + 1) * size)
            leaving = []
            for d in range(2):
                of_re = total[d * half:d * half + part]
                of_im = total[d * half + part:(d + 1) * half]
                leaving.append(
                    (of_re[:, :size] - of_im[:, size:], of_re[:, size:] + of_im[:, :size])
                )

            @pl.when(depth == 0)
            def _():
                for d in range(2):
                    re, im = reflected(*leaving[d], c_re[:, at], c_im[:, at])
                    stage[k, d, b, 0:part] = re
                    stage[k, d, b, part:half] = im

            @pl.when(depth == 1)
            def _():
                for d in range(2):
                    for c in range(2):
                        final[k, d, c, :, at] = leaving[d][c]

        @pl.when(depth == 0)
        def _():
            for d in range(2):
                leaving_across(k, d).start()
            for d in range(2):
                leaving_own(k, d).start()

        @pl.when(depth == 1)
        def _():
            return_copy(k).start()
            pltpu.make_async_copy(final.at[k, 1], out.at[k], store_o.at[k]).start()

    @pl.when(depth == 0)
    def _():
        for k in range(panels):
            for d in range(2):
                leaving_across(k, d).wait_send()
                leaving_own(k, d).wait_send()
            return_copy(k).wait_recv()

    @pl.when(depth == 1)
    def _():
        for k in range(panels):
            entering_own(k).wait_send()
            return_copy(k).wait_send()
            pltpu.make_async_copy(final.at[k, 1], out.at[k], store_o.at[k]).wait()

    entering_across(panels - 1).wait_send()

    @pl.when(has_onward)
    def _():
        for k in range(panels):
            for d in range(2):
                onward_copy(k, d).wait_send()


def per_device(sources, blocks, block_cols, refl_level, refl_coef):
    lat_count = lax.axis_size("lat")
    assert lax.axis_size("depth") == 2 and blocks.shape[0] == 1 and lat_count % 2 == 0
    panels, _, part, points = sources.shape
    _, rows, per_row, _, size, _ = blocks.shape
    half = 2 * part
    f32, bf16 = jnp.float32, jnp.bfloat16
    dma = pltpu.SemaphoreType.DMA
    anywhere = pl.BlockSpec(memory_space=pl.ANY)
    flops = 2 * 3 * 4 * panels * part * 2 * rows * per_row * size * size * 2
    return pl.pallas_call(
        functools.partial(kernel, lat_count),
        out_shape=jax.ShapeDtypeStruct(sources.shape, f32),
        in_specs=[
            anywhere,
            pl.BlockSpec(memory_space=pltpu.SMEM),
            anywhere,
            anywhere,
            anywhere,
        ],
        out_specs=anywhere,
        scratch_shapes=[
            pltpu.VMEM((rows, per_row, 2, size, size), f32),
            pltpu.VMEM((rows, per_row * size, 2 * size), bf16),
            pltpu.VMEM((rows, per_row * size, 2 * size), bf16),
            pltpu.VMEM((panels, 2, part, points), f32),
            pltpu.VMEM((1, points), jnp.int32),
            pltpu.VMEM((2, points), f32),
            pltpu.VMEM((panels, rows, half, size), f32),
            pltpu.VMEM((panels, 2, 3 * rows, half, size), f32),
            pltpu.VMEM((panels, 3 * rows, 4 * half, size), bf16),
            pltpu.VMEM((panels, 2, rows, half, size), f32),
            pltpu.VMEM((panels, 2, 2, part, points), f32),
            dma((rows,)), dma((panels,)), dma((2,)),
            dma((panels,)), dma((panels,)), dma((panels, 2)),
            dma((panels, 2)), dma((panels, 2)), dma((panels,)),
            dma((panels, 2)), dma((panels, 2)), dma((panels, 2)),
            dma((panels,)), dma((panels,)),
        ],
        compiler_params=pltpu.CompilerParams(
            collective_id=0, has_side_effects=True, vmem_limit_bytes=63 * 1024 * 1024
        ),
        cost_estimate=pl.CostEstimate(
            flops=flops, bytes_accessed=4 * (blocks.size + 2 * sources.size), transcendentals=0
        ),
    )(blocks, block_cols, sources, refl_level.reshape(1, points), refl_coef)


def solution(mesh):
    placed = (
        P("shot", None, "depth", "lat"),
        P(("shot", "depth"), "lat", None, None, None, None),
        P("depth", "lat", None),
        P("lat"),
        P(None, "lat"),
    )
    return jax.shard_map(
        per_device,
        mesh=mesh,
        in_specs=placed,
        out_specs=P("shot", None, "depth", "lat"),
        check_vma=False,
    )
```

```python
import functools

import jax
import jax.numpy as jnp
from jax import lax
from jax.experimental import pallas as pl
from jax.experimental.pallas import tpu as pltpu
from jax.sharding import PartitionSpec as P

MESH = pl.DeviceIdType.MESH


def split_bf16(value):
    high = value.astype(jnp.bfloat16)
    low = (value - high.astype(jnp.float32)).astype(jnp.bfloat16)
    return high, low


def kernel(
    lat_count, blocks, cols, cols_hbm, sources, level, coef, out,
    raw, w_hi, w_lo, src, lev, cf, field, parts, final, cols_in, cols_other,
    load_w, load_s, load_r, load_c, send_w, recv_w, send_i, recv_i,
    send_x, recv_x, send_z, recv_z, store_o,
):
    panels, _, part, points = sources.shape
    _, rows, per_row, _, size, _ = blocks.shape
    half = panels * part
    full = 2 * half
    depth = lax.axis_index("depth")
    lat = lax.axis_index("lat")
    odd = lax.rem(lat, 2)
    pair = lat + 1 - 2 * odd
    onward = lat + 2 - 4 * odd
    behind = lat - 2 + 4 * odd
    has_onward = jnp.logical_and(onward >= 0, onward < lat_count)
    has_behind = jnp.logical_and(behind >= 0, behind < lat_count)
    near = 2 * rows * (1 - odd)
    far = 2 * rows * odd

    weight_loads = [
        pltpu.make_async_copy(blocks.at[0, b], raw.at[depth, b], load_w.at[b])
        for b in range(rows)
    ]
    source_load = pltpu.make_async_copy(sources, src, load_s.at[0])
    refl_loads = [
        pltpu.make_async_copy(level, lev, load_r.at[0]),
        pltpu.make_async_copy(coef, cf, load_r.at[1]),
    ]
    for copy in refl_loads + [source_load] + weight_loads:
        copy.start()

    barrier = pltpu.get_barrier_semaphore()
    pl.semaphore_signal(barrier, device_id={"depth": 1 - depth, "lat": lat}, device_id_type=MESH)
    pl.semaphore_signal(barrier, device_id={"depth": depth, "lat": pair}, device_id_type=MESH)

    @pl.when(has_behind)
    def _():
        pl.semaphore_signal(barrier, device_id={"depth": depth, "lat": behind}, device_id_type=MESH)

    for copy in refl_loads:
        copy.wait()

    def coefficients(at):
        here = lev[...] == at
        zero = jnp.float32(0.0)
        return jnp.where(here, cf[0:1, :], zero), jnp.where(here, cf[1:2, :], zero)

    def reflected(re, im, c_re, c_im):
        return re + c_re * re - c_im * im, im + c_re * im + c_im * re

    def send(src_ref, dst_ref, send_sem, recv_sem, to_depth, to_lat):
        return pltpu.make_async_remote_copy(
            src_ref=src_ref, dst_ref=dst_ref, send_sem=send_sem, recv_sem=recv_sem,
            device_id={"depth": to_depth, "lat": to_lat}, device_id_type=MESH,
        )

    def across(l, b):
        return send(
            field.at[l, rows + b], field.at[l, far + b],
            send_x.at[l, b], recv_x.at[l, b], depth, pair,
        )

    def along(l, b):
        return send(
            field.at[l, near + b], field.at[l, far + b],
            send_z.at[l, b], recv_z.at[l, b], depth, onward,
        )

    def exchange(b):
        return send(
            blocks.at[0, b], raw.at[depth, b], send_w.at[b], recv_w.at[b], 1 - depth, lat,
        )

    def exchange_cols():
        return send(cols_hbm, cols_in, send_i.at[0], recv_i.at[0], 1 - depth, lat)

    def split_slot(l, slot):
        high, low = split_bf16(field[l, slot])
        parts[slot, 0:full] = high
        parts[slot, full:2 * full] = low

    def split_row(l, b):
        @pl.loop(0, per_row)
        def _(j):
            at = pl.ds(pl.multiple_of(j * size, size), size)
            for c in range(2):
                high, low = split_bf16(raw[l, b, j, c])
                w_hi[l, b, at, c * size:(c + 1) * size] = high
                w_lo[l, b, at, c * size:(c + 1) * size] = low

    def split_received(l, own):
        @pl.when(depth != own)
        def _():
            for b in range(rows):
                exchange(b).wait_recv()
                split_row(l, b)

    def finish_halo(l):
        for b in range(rows):
            split_slot(l, rows + b)
            split_slot(l, near + b)

        @pl.when(has_behind)
        def _():
            for b in range(rows):
                along(l, b).wait_recv()
                split_slot(l, far + b)

    def pass_on(l, b):
        across(l, b).wait_recv()

        @pl.when(has_onward)
        def _():
            along(l, b).start()

    base = (lat - 1) * rows

    def column(l, b, j):
        listed = jnp.where(depth == l, cols[0, b, j], cols_other[0, b, j])
        return jnp.clip(listed - base, 0, 3 * rows - 1)

    def row_of(l, b):
        picked = jnp.concatenate([parts[column(l, b, j)] for j in range(per_row)], axis=1)
        both = jnp.dot(picked, w_hi[l, b], preferred_element_type=jnp.float32)
        rest = jnp.dot(picked[:full], w_lo[l, b], preferred_element_type=jnp.float32)
        total = both[:full] + (both[full:] + rest)
        of_re, of_im = total[:half], total[half:]
        return of_re[:, :size] - of_im[:, size:], of_re[:, size:] + of_im[:, :size]

    c_re, c_im = coefficients(0)
    source_load.wait()
    for b in range(rows):
        at = slice(b * size, (b + 1) * size)
        for k in range(panels):
            re, im = reflected(src[k, 0, :, at], src[k, 1, :, at], c_re[:, at], c_im[:, at])
            field[0, rows + b, k * part:(k + 1) * part] = re
            field[0, rows + b, half + k * part:half + (k + 1) * part] = im
        if b == 0:
            pl.semaphore_wait(barrier, 2 + has_onward.astype(jnp.int32))
        across(0, b).start()
    exchange_cols().start()
    for b in range(rows):
        exchange(b).start()

    for b in range(rows):
        weight_loads[b].wait()
        split_row(depth, b)
        pass_on(0, b)
    exchange_cols().wait_recv()
    listed = pltpu.make_async_copy(cols_in, cols_other, load_c.at[0])
    listed.start()
    finish_halo(0)
    split_received(0, 0)
    listed.wait()

    c_re, c_im = coefficients(1)
    for b in range(rows):
        at = slice(b * size, (b + 1) * size)
        re, im = reflected(*row_of(0, b), c_re[:, at], c_im[:, at])
        field[1, rows + b, 0:half] = re
        field[1, rows + b, half:full] = im
        across(1, b).start()
    split_received(1, 1)
    for b in range(rows):
        pass_on(1, b)
    finish_halo(1)
    for b in range(rows):
        at = slice(b * size, (b + 1) * size)
        re, im = row_of(1, b)
        for k in range(panels):
            final[k, 0, :, at] = re[k * part:(k + 1) * part]
            final[k, 1, :, at] = im[k * part:(k + 1) * part]
    store = pltpu.make_async_copy(final, out, store_o.at[0])
    store.start()

    exchange_cols().wait_send()
    for b in range(rows):
        exchange(b).wait_send()
        for l in range(2):
            across(l, b).wait_send()

    @pl.when(has_onward)
    def _():
        for l in range(2):
            for b in range(rows):
                along(l, b).wait_send()

    store.wait()


def per_device(sources, blocks, block_cols, refl_level, refl_coef):
    lat_count = lax.axis_size("lat")
    assert lax.axis_size("depth") == 2 and blocks.shape[0] == 1 and lat_count % 2 == 0
    panels, _, part, points = sources.shape
    _, rows, per_row, _, size, _ = blocks.shape
    full = 2 * panels * part
    f32, bf16 = jnp.float32, jnp.bfloat16
    dma = pltpu.SemaphoreType.DMA
    anywhere = pl.BlockSpec(memory_space=pl.ANY)
    flops = 2 * 3 * 2 * full * rows * per_row * size * size * 2
    return pl.pallas_call(
        functools.partial(kernel, lat_count),
        out_shape=jax.ShapeDtypeStruct(sources.shape, f32),
        in_specs=[
            anywhere,
            pl.BlockSpec(memory_space=pltpu.SMEM),
            anywhere,
            anywhere,
            anywhere,
            anywhere,
        ],
        out_specs=anywhere,
        scratch_shapes=[
            pltpu.VMEM((2, rows, per_row, 2, size, size), f32),
            pltpu.VMEM((2, rows, per_row * size, 2 * size), bf16),
            pltpu.VMEM((2, rows, per_row * size, 2 * size), bf16),
            pltpu.VMEM((panels, 2, part, points), f32),
            pltpu.VMEM((1, points), jnp.int32),
            pltpu.VMEM((2, points), f32),
            pltpu.VMEM((2, 3 * rows, full, size), f32),
            pltpu.VMEM((3 * rows, 2 * full, size), bf16),
            pltpu.VMEM((panels, 2, part, points), f32),
            pltpu.VMEM(block_cols.shape, jnp.int32),
            pltpu.SMEM(block_cols.shape, jnp.int32),
            dma((rows,)), dma((1,)), dma((2,)), dma((1,)),
            dma((rows,)), dma((rows,)), dma((1,)), dma((1,)),
            dma((2, rows)), dma((2, rows)), dma((2, rows)), dma((2, rows)), dma((1,)),
        ],
        compiler_params=pltpu.CompilerParams(
            collective_id=0, has_side_effects=True, vmem_limit_bytes=63 * 1024 * 1024
        ),
        cost_estimate=pl.CostEstimate(
            flops=flops, bytes_accessed=4 * (blocks.size + 2 * sources.size), transcendentals=0
        ),
    )(blocks, block_cols, block_cols, sources, refl_level.reshape(1, points), refl_coef)


def solution(mesh):
    placed = (
        P("shot", None, "depth", "lat"),
        P(("shot", "depth"), "lat", None, None, None, None),
        P("depth", "lat", None),
        P("lat"),
        P(None, "lat"),
    )
    return jax.shard_map(
        per_device,
        mesh=mesh,
        in_specs=placed,
        out_specs=P("shot", None, "depth", "lat"),
        check_vma=False,
    )
```

```python
import functools

import jax
import jax.numpy as jnp
from jax import lax
from jax.experimental import pallas as pl
from jax.experimental.pallas import tpu as pltpu
from jax.sharding import PartitionSpec as P

MESH = pl.DeviceIdType.MESH


def split_bf16(value):
    high = value.astype(jnp.bfloat16)
    low = (value - high.astype(jnp.float32)).astype(jnp.bfloat16)
    return high, low


def kernel(
    lat_count, blocks, cols, cols_hbm, sources, level, coef, out,
    raw, w_hi, w_lo, src, lev, cf, field, parts, final, cols_in, cols_other,
    load_w, load_s, load_r, load_c, send_w, recv_w, send_i, recv_i,
    send_x, recv_x, send_z, recv_z, send_d, store_o,
):
    panels, _, part, points = sources.shape
    _, rows, per_row, _, size, _ = blocks.shape
    half = panels * part
    full = 2 * half
    relayed = rows - 1
    depth = lax.axis_index("depth")
    lat = lax.axis_index("lat")
    odd = lax.rem(lat, 2)
    pair = lat + 1 - 2 * odd
    onward = lat + 2 - 4 * odd
    behind = lat - 2 + 4 * odd
    diagonal = lat - 1 + 2 * odd
    has_onward = jnp.logical_and(onward >= 0, onward < lat_count)
    has_behind = jnp.logical_and(behind >= 0, behind < lat_count)
    near = 2 * rows * (1 - odd)
    far = 2 * rows * odd

    weight_loads = [
        pltpu.make_async_copy(blocks.at[0, b], raw.at[depth, b], load_w.at[b])
        for b in range(rows)
    ]
    source_load = pltpu.make_async_copy(sources, src, load_s.at[0])
    refl_loads = [
        pltpu.make_async_copy(level, lev, load_r.at[0]),
        pltpu.make_async_copy(coef, cf, load_r.at[1]),
    ]
    for copy in refl_loads + [source_load] + weight_loads:
        copy.start()

    barrier = pltpu.get_barrier_semaphore()
    pl.semaphore_signal(barrier, device_id={"depth": 1 - depth, "lat": lat}, device_id_type=MESH)
    pl.semaphore_signal(barrier, device_id={"depth": depth, "lat": pair}, device_id_type=MESH)

    @pl.when(has_behind)
    def _():
        pl.semaphore_signal(barrier, device_id={"depth": depth, "lat": behind}, device_id_type=MESH)
        pl.semaphore_signal(
            barrier, device_id={"depth": depth, "lat": diagonal}, device_id_type=MESH
        )

    for copy in refl_loads:
        copy.wait()

    def coefficients(at):
        here = lev[...] == at
        zero = jnp.float32(0.0)
        return jnp.where(here, cf[0:1, :], zero), jnp.where(here, cf[1:2, :], zero)

    def reflected(re, im, c_re, c_im):
        return re + c_re * re - c_im * im, im + c_re * im + c_im * re

    def send(src_ref, dst_ref, send_sem, recv_sem, to_depth, to_lat):
        return pltpu.make_async_remote_copy(
            src_ref=src_ref, dst_ref=dst_ref, send_sem=send_sem, recv_sem=recv_sem,
            device_id={"depth": to_depth, "lat": to_lat}, device_id_type=MESH,
        )

    def across(l, b):
        return send(
            field.at[l, rows + b], field.at[l, far + b],
            send_x.at[l, b], recv_x.at[l, b], depth, pair,
        )

    def along(l, b):
        return send(
            field.at[l, near + b], field.at[l, far + b],
            send_z.at[l, b], recv_z.at[l, b], depth, onward,
        )

    def direct(l, b):
        return send(
            field.at[l, rows + b], field.at[l, near + b],
            send_d.at[l, b - relayed], recv_z.at[l, b], depth, diagonal,
        )

    def start_halo(l, b):
        across(l, b).start()
        if b >= relayed:

            @pl.when(has_behind)
            def _():
                direct(l, b).start()

    def exchange(b):
        return send(
            blocks.at[0, b], raw.at[depth, b], send_w.at[b], recv_w.at[b], 1 - depth, lat,
        )

    def exchange_cols():
        return send(cols_hbm, cols_in, send_i.at[0], recv_i.at[0], 1 - depth, lat)

    def split_slot(l, slot):
        high, low = split_bf16(field[l, slot])
        parts[l, slot, 0:full] = high
        parts[l, slot, full:2 * full] = low

    def split_row(l, b):
        @pl.loop(0, per_row)
        def _(j):
            at = pl.ds(pl.multiple_of(j * size, size), size)
            for c in range(2):
                high, low = split_bf16(raw[l, b, j, c])
                w_hi[l, b, at, c * size:(c + 1) * size] = high
                w_lo[l, b, at, c * size:(c + 1) * size] = low

    def split_received(l, b, own):
        @pl.when(depth != own)
        def _():
            exchange(b).wait_recv()
            split_row(l, b)

    def finish_halo(l):
        @pl.when(has_behind)
        def _():
            for b in range(rows):
                along(l, b).wait_recv()
                split_slot(l, far + b)

    def pass_on(l, b):
        across(l, b).wait_recv()
        if b < relayed:

            @pl.when(has_onward)
            def _():
                along(l, b).start()

        split_slot(l, near + b)

    base = (lat - 1) * rows

    def column(l, b, j):
        listed = jnp.where(depth == l, cols[0, b, j], cols_other[0, b, j])
        return jnp.clip(listed - base, 0, 3 * rows - 1)

    def row_of(l, b):
        picked = jnp.concatenate([parts[l, column(l, b, j)] for j in range(per_row)], axis=1)
        both = jnp.dot(picked, w_hi[l, b], preferred_element_type=jnp.float32)
        rest = jnp.dot(picked[:full], w_lo[l, b], preferred_element_type=jnp.float32)
        total = both[:full] + (both[full:] + rest)
        of_re, of_im = total[:half], total[half:]
        return of_re[:, :size] - of_im[:, size:], of_re[:, size:] + of_im[:, :size]

    c_re, c_im = coefficients(0)
    source_load.wait()
    for b in range(rows):
        at = slice(b * size, (b + 1) * size)
        for k in range(panels):
            re, im = reflected(src[k, 0, :, at], src[k, 1, :, at], c_re[:, at], c_im[:, at])
            field[0, rows + b, k * part:(k + 1) * part] = re
            field[0, rows + b, half + k * part:half + (k + 1) * part] = im
        if b == 0:
            pl.semaphore_wait(barrier, 2 + has_onward.astype(jnp.int32) + has_behind.astype(jnp.int32))
        start_halo(0, b)
    exchange_cols().start()
    for b in range(rows):
        exchange(b).start()

    for b in range(rows):
        split_slot(0, rows + b)
    for b in range(rows):
        weight_loads[b].wait()
        split_row(depth, b)
        pass_on(0, b)
    exchange_cols().wait_recv()
    listed = pltpu.make_async_copy(cols_in, cols_other, load_c.at[0])
    listed.start()
    for b in range(rows):
        split_received(0, b, 0)
    listed.wait()
    finish_halo(0)

    c_re, c_im = coefficients(1)
    for b in range(rows):
        at = slice(b * size, (b + 1) * size)
        re, im = reflected(*row_of(0, b), c_re[:, at], c_im[:, at])
        field[1, rows + b, 0:half] = re
        field[1, rows + b, half:full] = im
        start_halo(1, b)
    for b in range(rows):
        split_slot(1, rows + b)
    for b in range(rows):
        split_received(1, b, 1)
        pass_on(1, b)
    finish_halo(1)
    for b in range(rows):
        at = slice(b * size, (b + 1) * size)
        re, im = row_of(1, b)
        for k in range(panels):
            final[k, 0, :, at] = re[k * part:(k + 1) * part]
            final[k, 1, :, at] = im[k * part:(k + 1) * part]
    store = pltpu.make_async_copy(final, out, store_o.at[0])
    store.start()

    exchange_cols().wait_send()
    for b in range(rows):
        exchange(b).wait_send()
        for l in range(2):
            across(l, b).wait_send()

    @pl.when(has_onward)
    def _():
        for l in range(2):
            for b in range(relayed):
                along(l, b).wait_send()

    @pl.when(has_behind)
    def _():
        for l in range(2):
            for b in range(relayed, rows):
                direct(l, b).wait_send()

    store.wait()


def per_device(sources, blocks, block_cols, refl_level, refl_coef):
    lat_count = lax.axis_size("lat")
    assert lax.axis_size("depth") == 2 and blocks.shape[0] == 1 and lat_count % 2 == 0
    panels, _, part, points = sources.shape
    _, rows, per_row, _, size, _ = blocks.shape
    full = 2 * panels * part
    f32, bf16 = jnp.float32, jnp.bfloat16
    dma = pltpu.SemaphoreType.DMA
    anywhere = pl.BlockSpec(memory_space=pl.ANY)
    flops = 2 * 3 * 2 * full * rows * per_row * size * size * 2
    return pl.pallas_call(
        functools.partial(kernel, lat_count),
        out_shape=jax.ShapeDtypeStruct(sources.shape, f32),
        in_specs=[
            anywhere,
            pl.BlockSpec(memory_space=pltpu.SMEM),
            anywhere,
            anywhere,
            anywhere,
            anywhere,
        ],
        out_specs=anywhere,
        scratch_shapes=[
            pltpu.VMEM((2, rows, per_row, 2, size, size), f32),
            pltpu.VMEM((2, rows, per_row * size, 2 * size), bf16),
            pltpu.VMEM((2, rows, per_row * size, 2 * size), bf16),
            pltpu.VMEM((panels, 2, part, points), f32),
            pltpu.VMEM((1, points), jnp.int32),
            pltpu.VMEM((2, points), f32),
            pltpu.VMEM((2, 3 * rows, full, size), f32),
            pltpu.VMEM((2, 3 * rows, 2 * full, size), bf16),
            pltpu.VMEM((panels, 2, part, points), f32),
            pltpu.VMEM(block_cols.shape, jnp.int32),
            pltpu.SMEM(block_cols.shape, jnp.int32),
            dma((rows,)), dma((1,)), dma((2,)), dma((1,)),
            dma((rows,)), dma((rows,)), dma((1,)), dma((1,)),
            dma((2, rows)), dma((2, rows)), dma((2, rows)), dma((2, rows)), dma((2, rows)), dma((1,)),
        ],
        compiler_params=pltpu.CompilerParams(
            collective_id=0, has_side_effects=True, vmem_limit_bytes=63 * 1024 * 1024
        ),
        cost_estimate=pl.CostEstimate(
            flops=flops, bytes_accessed=4 * (blocks.size + 2 * sources.size), transcendentals=0
        ),
    )(blocks, block_cols, block_cols, sources, refl_level.reshape(1, points), refl_coef)


def solution(mesh):
    placed = (
        P("shot", None, "depth", "lat"),
        P(("shot", "depth"), "lat", None, None, None, None),
        P("depth", "lat", None),
        P("lat"),
        P(None, "lat"),
    )
    return jax.shard_map(
        per_device,
        mesh=mesh,
        in_specs=placed,
        out_specs=P("shot", None, "depth", "lat"),
        check_vma=False,
    )
```

```python
import functools

import jax
import jax.numpy as jnp
from jax import lax
from jax.experimental import pallas as pl
from jax.experimental.pallas import tpu as pltpu
from jax.sharding import PartitionSpec as P

MESH = pl.DeviceIdType.MESH


def split_bf16(value):
    high = value.astype(jnp.bfloat16)
    low = (value - high.astype(jnp.float32)).astype(jnp.bfloat16)
    return high, low


def kernel(
    lat_count, blocks, cols, cols_hbm, sources, level, coef, out,
    raw, w_hi, w_lo, src, lev, cf, field, parts, final, cols_in, cols_other,
    load_w, load_s, load_r, load_c, send_w, recv_w, send_i, recv_i,
    send_x, recv_x, send_z, recv_z, send_d, store_o,
):
    panels, _, part, points = sources.shape
    _, rows, per_row, _, size, _ = blocks.shape
    half = panels * part
    full = 2 * half
    relayed = rows - 1
    depth = lax.axis_index("depth")
    lat = lax.axis_index("lat")
    odd = lax.rem(lat, 2)
    pair = lat + 1 - 2 * odd
    onward = lat + 2 - 4 * odd
    behind = lat - 2 + 4 * odd
    diagonal = lat - 1 + 2 * odd
    has_onward = jnp.logical_and(onward >= 0, onward < lat_count)
    has_behind = jnp.logical_and(behind >= 0, behind < lat_count)
    near = 2 * rows * (1 - odd)
    far = 2 * rows * odd

    weight_loads = [
        pltpu.make_async_copy(blocks.at[0, b], raw.at[depth, b], load_w.at[b])
        for b in range(rows)
    ]
    source_load = pltpu.make_async_copy(sources, src, load_s.at[0])
    refl_loads = [
        pltpu.make_async_copy(level, lev, load_r.at[0]),
        pltpu.make_async_copy(coef, cf, load_r.at[1]),
    ]
    for copy in refl_loads + [source_load] + weight_loads:
        copy.start()

    barrier = pltpu.get_barrier_semaphore()
    pl.semaphore_signal(barrier, device_id={"depth": 1 - depth, "lat": lat}, device_id_type=MESH)
    pl.semaphore_signal(barrier, device_id={"depth": depth, "lat": pair}, device_id_type=MESH)

    @pl.when(has_behind)
    def _():
        pl.semaphore_signal(barrier, device_id={"depth": depth, "lat": behind}, device_id_type=MESH)
        pl.semaphore_signal(
            barrier, device_id={"depth": depth, "lat": diagonal}, device_id_type=MESH
        )

    for copy in refl_loads:
        copy.wait()

    def coefficients(at):
        here = lev[...] == at
        zero = jnp.float32(0.0)
        return jnp.where(here, cf[0:1, :], zero), jnp.where(here, cf[1:2, :], zero)

    def reflected(re, im, c_re, c_im):
        return re + c_re * re - c_im * im, im + c_re * im + c_im * re

    def send(src_ref, dst_ref, send_sem, recv_sem, to_depth, to_lat):
        return pltpu.make_async_remote_copy(
            src_ref=src_ref, dst_ref=dst_ref, send_sem=send_sem, recv_sem=recv_sem,
            device_id={"depth": to_depth, "lat": to_lat}, device_id_type=MESH,
        )

    def across(l, b):
        return send(
            field.at[l, rows + b], field.at[l, far + b],
            send_x.at[l, b], recv_x.at[l, b], depth, pair,
        )

    def along(l, b):
        return send(
            field.at[l, near + b], field.at[l, far + b],
            send_z.at[l, b], recv_z.at[l, b], depth, onward,
        )

    def direct(l, b):
        return send(
            field.at[l, rows + b], field.at[l, near + b],
            send_d.at[l, b - relayed], recv_z.at[l, b], depth, diagonal,
        )

    def start_halo(l, b):
        across(l, b).start()
        if b >= relayed:

            @pl.when(has_behind)
            def _():
                direct(l, b).start()

    def exchange(b):
        return send(
            blocks.at[0, b], raw.at[depth, b], send_w.at[b], recv_w.at[b], 1 - depth, lat,
        )

    def exchange_cols():
        return send(cols_hbm, cols_in, send_i.at[0], recv_i.at[0], 1 - depth, lat)

    def split_slot(l, slot):
        high, low = split_bf16(field[l, slot])
        parts[l, slot, 0:full] = high
        parts[l, slot, full:2 * full] = low

    def split_row(l, b):
        for j in range(per_row):
            at = slice(j * size, (j + 1) * size)
            for c in range(2):
                high, low = split_bf16(raw[l, b, j, c])
                w_hi[l, b, at, c * size:(c + 1) * size] = high
                w_lo[l, b, at, c * size:(c + 1) * size] = low

    def split_received(b):
        exchange(b).wait_recv()
        split_row(1 - depth, b)

    def finish_halo(l):
        @pl.when(has_behind)
        def _():
            for b in range(rows):
                along(l, b).wait_recv()
                split_slot(l, far + b)

    def pass_on(l, b):
        across(l, b).wait_recv()
        if b < relayed:

            @pl.when(has_onward)
            def _():
                along(l, b).start()

        split_slot(l, near + b)

    base = (lat - 1) * rows

    def column(l, b, j):
        listed = jnp.where(depth == l, cols[0, b, j], cols_other[0, b, j])
        return jnp.clip(listed - base, 0, 3 * rows - 1)

    def row_of(l, b):
        picked = jnp.concatenate([parts[l, column(l, b, j)] for j in range(per_row)], axis=1)
        both = jnp.dot(picked, w_hi[l, b], preferred_element_type=jnp.float32)
        rest = jnp.dot(picked[:full], w_lo[l, b], preferred_element_type=jnp.float32)
        total = both[:full] + (both[full:] + rest)
        of_re, of_im = total[:half], total[half:]
        return of_re[:, :size] - of_im[:, size:], of_re[:, size:] + of_im[:, :size]

    c_re, c_im = coefficients(0)
    source_load.wait()
    for b in range(rows):
        at = slice(b * size, (b + 1) * size)
        for k in range(panels):
            re, im = reflected(src[k, 0, :, at], src[k, 1, :, at], c_re[:, at], c_im[:, at])
            field[0, rows + b, k * part:(k + 1) * part] = re
            field[0, rows + b, half + k * part:half + (k + 1) * part] = im
        if b == 0:
            pl.semaphore_wait(barrier, 2 + has_onward.astype(jnp.int32) + has_behind.astype(jnp.int32))
        start_halo(0, b)
    exchange_cols().start()
    for b in range(rows):
        exchange(b).start()

    for b in range(rows):
        split_slot(0, rows + b)
    for b in range(rows):
        weight_loads[b].wait()
        split_row(depth, b)
        if b >= rows // 2:
            pass_on(0, b - rows // 2)
    early = rows // 2
    for b in range(rows - rows // 2, rows):
        pass_on(0, b)
    for b in range(early):
        split_received(b)
    exchange_cols().wait_recv()
    listed = pltpu.make_async_copy(cols_in, cols_other, load_c.at[0])
    listed.start()

    @pl.when(depth == 1)
    def _():
        for b in range(early, rows):
            split_received(b)

    listed.wait()
    finish_halo(0)

    c_re, c_im = coefficients(1)
    for b in range(rows):
        at = slice(b * size, (b + 1) * size)
        re, im = reflected(*row_of(0, b), c_re[:, at], c_im[:, at])
        field[1, rows + b, 0:half] = re
        field[1, rows + b, half:full] = im
        start_halo(1, b)
    for b in range(rows):
        split_slot(1, rows + b)

    @pl.when(depth == 0)
    def _():
        for b in range(early, rows):
            split_received(b)

    for b in range(rows):
        pass_on(1, b)
    finish_halo(1)
    for b in range(rows):
        at = slice(b * size, (b + 1) * size)
        re, im = row_of(1, b)
        for k in range(panels):
            final[k, 0, :, at] = re[k * part:(k + 1) * part]
            final[k, 1, :, at] = im[k * part:(k + 1) * part]
    store = pltpu.make_async_copy(final, out, store_o.at[0])
    store.start()

    exchange_cols().wait_send()
    for b in range(rows):
        exchange(b).wait_send()
        for l in range(2):
            across(l, b).wait_send()

    @pl.when(has_onward)
    def _():
        for l in range(2):
            for b in range(relayed):
                along(l, b).wait_send()

    @pl.when(has_behind)
    def _():
        for l in range(2):
            for b in range(relayed, rows):
                direct(l, b).wait_send()

    store.wait()


def per_device(sources, blocks, block_cols, refl_level, refl_coef):
    lat_count = lax.axis_size("lat")
    assert lax.axis_size("depth") == 2 and blocks.shape[0] == 1 and lat_count % 2 == 0
    panels, _, part, points = sources.shape
    _, rows, per_row, _, size, _ = blocks.shape
    full = 2 * panels * part
    f32, bf16 = jnp.float32, jnp.bfloat16
    dma = pltpu.SemaphoreType.DMA
    anywhere = pl.BlockSpec(memory_space=pl.ANY)
    flops = 2 * 3 * 2 * full * rows * per_row * size * size * 2
    return pl.pallas_call(
        functools.partial(kernel, lat_count),
        out_shape=jax.ShapeDtypeStruct(sources.shape, f32),
        in_specs=[
            anywhere,
            pl.BlockSpec(memory_space=pltpu.SMEM),
            anywhere,
            anywhere,
            anywhere,
            anywhere,
        ],
        out_specs=anywhere,
        scratch_shapes=[
            pltpu.VMEM((2, rows, per_row, 2, size, size), f32),
            pltpu.VMEM((2, rows, per_row * size, 2 * size), bf16),
            pltpu.VMEM((2, rows, per_row * size, 2 * size), bf16),
            pltpu.VMEM((panels, 2, part, points), f32),
            pltpu.VMEM((1, points), jnp.int32),
            pltpu.VMEM((2, points), f32),
            pltpu.VMEM((2, 3 * rows, full, size), f32),
            pltpu.VMEM((2, 3 * rows, 2 * full, size), bf16),
            pltpu.VMEM((panels, 2, part, points), f32),
            pltpu.VMEM(block_cols.shape, jnp.int32),
            pltpu.SMEM(block_cols.shape, jnp.int32),
            dma((rows,)), dma((1,)), dma((2,)), dma((1,)),
            dma((rows,)), dma((rows,)), dma((1,)), dma((1,)),
            dma((2, rows)), dma((2, rows)), dma((2, rows)), dma((2, rows)), dma((2, rows)), dma((1,)),
        ],
        compiler_params=pltpu.CompilerParams(
            collective_id=0, has_side_effects=True, vmem_limit_bytes=63 * 1024 * 1024
        ),
        cost_estimate=pl.CostEstimate(
            flops=flops, bytes_accessed=4 * (blocks.size + 2 * sources.size), transcendentals=0
        ),
    )(blocks, block_cols, block_cols, sources, refl_level.reshape(1, points), refl_coef)


def solution(mesh):
    placed = (
        P("shot", None, "depth", "lat"),
        P(("shot", "depth"), "lat", None, None, None, None),
        P("depth", "lat", None),
        P("lat"),
        P(None, "lat"),
    )
    return jax.shard_map(
        per_device,
        mesh=mesh,
        in_specs=placed,
        out_specs=P("shot", None, "depth", "lat"),
        check_vma=False,
    )
```

```python
import functools

import jax
import jax.numpy as jnp
from jax import lax
from jax.experimental import pallas as pl
from jax.experimental.pallas import tpu as pltpu
from jax.sharding import PartitionSpec as P

MESH = pl.DeviceIdType.MESH


def split_bf16(value):
    high = value.astype(jnp.bfloat16)
    low = (value - high.astype(jnp.float32)).astype(jnp.bfloat16)
    return high, low


def kernel(
    lat_count, blocks, cols, cols_hbm, sources, level, coef, out,
    raw, w_hi, w_lo, src, lev, cf, field, parts, final, cols_in, cols_other,
    load_w, load_s, load_r, load_c, send_w, recv_w, send_i, recv_i,
    send_x, recv_x, send_z, recv_z, store_o,
):
    panels, _, part, points = sources.shape
    _, rows, per_row, _, size, _ = blocks.shape
    half = panels * part
    full = 2 * half
    depth = lax.axis_index("depth")
    lat = lax.axis_index("lat")
    odd = lax.rem(lat, 2)
    pair = lat + 1 - 2 * odd
    onward = lat + 2 - 4 * odd
    behind = lat - 2 + 4 * odd
    has_onward = jnp.logical_and(onward >= 0, onward < lat_count)
    has_behind = jnp.logical_and(behind >= 0, behind < lat_count)
    near = 2 * rows * (1 - odd)
    far = 2 * rows * odd

    weight_loads = [
        pltpu.make_async_copy(blocks.at[0, b], raw.at[depth, b], load_w.at[b])
        for b in range(rows)
    ]
    source_load = pltpu.make_async_copy(sources, src, load_s.at[0])
    refl_loads = [
        pltpu.make_async_copy(level, lev, load_r.at[0]),
        pltpu.make_async_copy(coef, cf, load_r.at[1]),
    ]
    for copy in refl_loads + [source_load] + weight_loads:
        copy.start()

    barrier = pltpu.get_barrier_semaphore()
    pl.semaphore_signal(barrier, device_id={"depth": 1 - depth, "lat": lat}, device_id_type=MESH)
    pl.semaphore_signal(barrier, device_id={"depth": depth, "lat": pair}, device_id_type=MESH)

    @pl.when(has_behind)
    def _():
        pl.semaphore_signal(barrier, device_id={"depth": depth, "lat": behind}, device_id_type=MESH)

    for copy in refl_loads:
        copy.wait()

    def coefficients(at):
        here = lev[...] == at
        zero = jnp.float32(0.0)
        return jnp.where(here, cf[0:1, :], zero), jnp.where(here, cf[1:2, :], zero)

    def reflected(re, im, c_re, c_im):
        return re + c_re * re - c_im * im, im + c_re * im + c_im * re

    def send(src_ref, dst_ref, send_sem, recv_sem, to_depth, to_lat):
        return pltpu.make_async_remote_copy(
            src_ref=src_ref, dst_ref=dst_ref, send_sem=send_sem, recv_sem=recv_sem,
            device_id={"depth": to_depth, "lat": to_lat}, device_id_type=MESH,
        )

    def across(l, b):
        return send(
            field.at[l, rows + b], field.at[l, far + b],
            send_x.at[l, b], recv_x.at[l, b], depth, pair,
        )

    def along(l, b):
        return send(
            field.at[l, near + b], field.at[l, far + b],
            send_z.at[l, b], recv_z.at[l, b], depth, onward,
        )

    def exchange(b):
        return send(
            blocks.at[0, b], raw.at[depth, b], send_w.at[b], recv_w.at[b], 1 - depth, lat,
        )

    def exchange_cols():
        return send(cols_hbm, cols_in, send_i.at[0], recv_i.at[0], 1 - depth, lat)

    def split_slot(l, slot):
        high, low = split_bf16(field[l, slot])
        parts[l, slot, 0:full] = high
        parts[l, slot, full:2 * full] = low

    def split_row(l, b):
        for j in range(per_row):
            at = slice(j * size, (j + 1) * size)
            for c in range(2):
                high, low = split_bf16(raw[l, b, j, c])
                w_hi[l, b, at, c * size:(c + 1) * size] = high
                w_lo[l, b, at, c * size:(c + 1) * size] = low

    def split_received(b):
        exchange(b).wait_recv()
        split_row(1 - depth, b)

    def finish_halo(l):
        @pl.when(has_behind)
        def _():
            for b in range(rows):
                along(l, b).wait_recv()
                split_slot(l, far + b)

    def pass_on(l, b):
        across(l, b).wait_recv()

        @pl.when(has_onward)
        def _():
            along(l, b).start()

        split_slot(l, near + b)

    base = (lat - 1) * rows

    def column(l, b, j):
        listed = jnp.where(depth == l, cols[0, b, j], cols_other[0, b, j])
        return jnp.clip(listed - base, 0, 3 * rows - 1)

    def row_of(l, b):
        picked = jnp.concatenate([parts[l, column(l, b, j)] for j in range(per_row)], axis=1)
        both = jnp.dot(picked, w_hi[l, b], preferred_element_type=jnp.float32)
        rest = jnp.dot(picked[:full], w_lo[l, b], preferred_element_type=jnp.float32)
        total = both[:full] + (both[full:] + rest)
        of_re, of_im = total[:half], total[half:]
        return of_re[:, :size] - of_im[:, size:], of_re[:, size:] + of_im[:, :size]

    c_re, c_im = coefficients(0)
    source_load.wait()
    for b in range(rows):
        at = slice(b * size, (b + 1) * size)
        for k in range(panels):
            re, im = reflected(src[k, 0, :, at], src[k, 1, :, at], c_re[:, at], c_im[:, at])
            field[0, rows + b, k * part:(k + 1) * part] = re
            field[0, rows + b, half + k * part:half + (k + 1) * part] = im
        if b == 0:
            pl.semaphore_wait(barrier, 2 + has_onward.astype(jnp.int32))
        across(0, b).start()
    exchange_cols().start()
    for b in range(rows):
        exchange(b).start()

    for b in range(rows):
        split_slot(0, rows + b)
    for b in range(rows):
        weight_loads[b].wait()
        split_row(depth, b)
        if b >= rows // 2:
            pass_on(0, b - rows // 2)
    early = rows // 2
    for b in range(rows - rows // 2, rows):
        pass_on(0, b)
    for b in range(early):
        split_received(b)
    exchange_cols().wait_recv()
    listed = pltpu.make_async_copy(cols_in, cols_other, load_c.at[0])
    listed.start()

    @pl.when(depth == 1)
    def _():
        for b in range(early, rows):
            split_received(b)

    listed.wait()
    finish_halo(0)

    c_re, c_im = coefficients(1)
    for b in range(rows):
        at = slice(b * size, (b + 1) * size)
        re, im = reflected(*row_of(0, b), c_re[:, at], c_im[:, at])
        field[1, rows + b, 0:half] = re
        field[1, rows + b, half:full] = im
        across(1, b).start()
    for b in range(rows):
        split_slot(1, rows + b)

    @pl.when(depth == 0)
    def _():
        for b in range(early, rows):
            split_received(b)

    for b in range(rows):
        pass_on(1, b)
    finish_halo(1)
    for b in range(rows):
        at = slice(b * size, (b + 1) * size)
        re, im = row_of(1, b)
        for k in range(panels):
            final[k, 0, :, at] = re[k * part:(k + 1) * part]
            final[k, 1, :, at] = im[k * part:(k + 1) * part]
    store = pltpu.make_async_copy(final, out, store_o.at[0])
    store.start()

    exchange_cols().wait_send()
    for b in range(rows):
        exchange(b).wait_send()
        for l in range(2):
            across(l, b).wait_send()

    @pl.when(has_onward)
    def _():
        for l in range(2):
            for b in range(rows):
                along(l, b).wait_send()

    store.wait()


def per_device(sources, blocks, block_cols, refl_level, refl_coef):
    lat_count = lax.axis_size("lat")
    assert lax.axis_size("depth") == 2 and blocks.shape[0] == 1 and lat_count % 2 == 0
    panels, _, part, points = sources.shape
    _, rows, per_row, _, size, _ = blocks.shape
    full = 2 * panels * part
    f32, bf16 = jnp.float32, jnp.bfloat16
    dma = pltpu.SemaphoreType.DMA
    anywhere = pl.BlockSpec(memory_space=pl.ANY)
    flops = 2 * 3 * 2 * full * rows * per_row * size * size * 2
    return pl.pallas_call(
        functools.partial(kernel, lat_count),
        out_shape=jax.ShapeDtypeStruct(sources.shape, f32),
        in_specs=[
            anywhere,
            pl.BlockSpec(memory_space=pltpu.SMEM),
            anywhere,
            anywhere,
            anywhere,
            anywhere,
        ],
        out_specs=anywhere,
        scratch_shapes=[
            pltpu.VMEM((2, rows, per_row, 2, size, size), f32),
            pltpu.VMEM((2, rows, per_row * size, 2 * size), bf16),
            pltpu.VMEM((2, rows, per_row * size, 2 * size), bf16),
            pltpu.VMEM((panels, 2, part, points), f32),
            pltpu.VMEM((1, points), jnp.int32),
            pltpu.VMEM((2, points), f32),
            pltpu.VMEM((2, 3 * rows, full, size), f32),
            pltpu.VMEM((2, 3 * rows, 2 * full, size), bf16),
            pltpu.VMEM((panels, 2, part, points), f32),
            pltpu.VMEM(block_cols.shape, jnp.int32),
            pltpu.SMEM(block_cols.shape, jnp.int32),
            dma((rows,)), dma((1,)), dma((2,)), dma((1,)),
            dma((rows,)), dma((rows,)), dma((1,)), dma((1,)),
            dma((2, rows)), dma((2, rows)), dma((2, rows)), dma((2, rows)), dma((1,)),
        ],
        compiler_params=pltpu.CompilerParams(
            collective_id=0, has_side_effects=True, vmem_limit_bytes=63 * 1024 * 1024
        ),
        cost_estimate=pl.CostEstimate(
            flops=flops, bytes_accessed=4 * (blocks.size + 2 * sources.size), transcendentals=0
        ),
    )(blocks, block_cols, block_cols, sources, refl_level.reshape(1, points), refl_coef)


def solution(mesh):
    placed = (
        P("shot", None, "depth", "lat"),
        P(("shot", "depth"), "lat", None, None, None, None),
        P("depth", "lat", None),
        P("lat"),
        P(None, "lat"),
    )
    return jax.shard_map(
        per_device,
        mesh=mesh,
        in_specs=placed,
        out_specs=P("shot", None, "depth", "lat"),
        check_vma=False,
    )
```

```python
import functools

import jax
import jax.numpy as jnp
from jax import lax
from jax.experimental import pallas as pl
from jax.experimental.pallas import tpu as pltpu
from jax.sharding import PartitionSpec as P

MESH = pl.DeviceIdType.MESH


def split_bf16(value):
    high = value.astype(jnp.bfloat16)
    low = (value - high.astype(jnp.float32)).astype(jnp.bfloat16)
    return high, low


def kernel(
    lat_count, blocks, cols, cols_hbm, sources, level, coef, out,
    raw, w_hi, w_lo, src, lev, cf, field, parts, final, cols_in, cols_other,
    load_w, load_s, load_r, load_c, send_w, recv_w, send_i, recv_i,
    send_x, recv_x, send_z, recv_z, store_o,
):
    panels, _, part, points = sources.shape
    _, rows, per_row, _, size, _ = blocks.shape
    half = panels * part
    full = 2 * half
    depth = lax.axis_index("depth")
    lat = lax.axis_index("lat")
    odd = lax.rem(lat, 2)
    pair = lat + 1 - 2 * odd
    onward = lat + 2 - 4 * odd
    behind = lat - 2 + 4 * odd
    has_onward = jnp.logical_and(onward >= 0, onward < lat_count)
    has_behind = jnp.logical_and(behind >= 0, behind < lat_count)
    near = 2 * rows * (1 - odd)
    far = 2 * rows * odd

    weight_loads = [
        pltpu.make_async_copy(blocks.at[0, b], raw.at[depth, b], load_w.at[b])
        for b in range(rows)
    ]
    source_load = pltpu.make_async_copy(sources, src, load_s.at[0])
    refl_loads = [
        pltpu.make_async_copy(level, lev, load_r.at[0]),
        pltpu.make_async_copy(coef, cf, load_r.at[1]),
    ]
    for copy in refl_loads + [source_load] + weight_loads:
        copy.start()

    barrier = pltpu.get_barrier_semaphore()
    pl.semaphore_signal(barrier, device_id={"depth": 1 - depth, "lat": lat}, device_id_type=MESH)
    pl.semaphore_signal(barrier, device_id={"depth": depth, "lat": pair}, device_id_type=MESH)

    @pl.when(has_behind)
    def _():
        pl.semaphore_signal(barrier, device_id={"depth": depth, "lat": behind}, device_id_type=MESH)

    for copy in refl_loads:
        copy.wait()

    def coefficients(at):
        here = lev[...] == at
        zero = jnp.float32(0.0)
        return jnp.where(here, cf[0:1, :], zero), jnp.where(here, cf[1:2, :], zero)

    def reflected(re, im, c_re, c_im):
        return re + c_re * re - c_im * im, im + c_re * im + c_im * re

    def send(src_ref, dst_ref, send_sem, recv_sem, to_depth, to_lat):
        return pltpu.make_async_remote_copy(
            src_ref=src_ref, dst_ref=dst_ref, send_sem=send_sem, recv_sem=recv_sem,
            device_id={"depth": to_depth, "lat": to_lat}, device_id_type=MESH,
        )

    def across(l, b):
        return send(
            field.at[l, rows + b], field.at[l, far + b],
            send_x.at[l, b], recv_x.at[l, b], depth, pair,
        )

    def along(l, b):
        return send(
            field.at[l, near + b], field.at[l, far + b],
            send_z.at[l, b], recv_z.at[l, b], depth, onward,
        )

    def exchange(b):
        return send(
            blocks.at[0, b], raw.at[depth, b], send_w.at[b], recv_w.at[b], 1 - depth, lat,
        )

    def exchange_cols():
        return send(cols_hbm, cols_in, send_i.at[0], recv_i.at[0], 1 - depth, lat)

    def split_slot(l, slot):
        high, low = split_bf16(field[l, slot])
        parts[l, slot, 0:full] = high
        parts[l, slot, full:2 * full] = low

    def split_row(l, b):
        for j in range(per_row):
            at = slice(j * size, (j + 1) * size)
            for c in range(2):
                high, low = split_bf16(raw[l, b, j, c])
                w_hi[l, b, at, c * size:(c + 1) * size] = high
                w_lo[l, b, at, c * size:(c + 1) * size] = low

    def split_received(b):
        exchange(b).wait_recv()
        split_row(1 - depth, b)

    def finish_halo(l):
        @pl.when(has_behind)
        def _():
            for b in range(rows):
                along(l, b).wait_recv()
                split_slot(l, far + b)

    def pass_on(l, b):
        across(l, b).wait_recv()

        @pl.when(has_onward)
        def _():
            along(l, b).start()

        split_slot(l, near + b)

    base = (lat - 1) * rows

    def column(l, b, j):
        listed = jnp.where(depth == l, cols[0, b, j], cols_other[0, b, j])
        return jnp.clip(listed - base, 0, 3 * rows - 1)

    def row_of(l, b):
        picked = jnp.concatenate([parts[l, column(l, b, j)] for j in range(per_row)], axis=1)
        both = jnp.dot(picked, w_hi[l, b], preferred_element_type=jnp.float32)
        rest = jnp.dot(picked[:full], w_lo[l, b], preferred_element_type=jnp.float32)
        total = both[:full] + (both[full:] + rest)
        of_re, of_im = total[:half], total[half:]
        return of_re[:, :size] - of_im[:, size:], of_re[:, size:] + of_im[:, :size]

    def store(b):
        at = pl.ds(b * size, size)
        return pltpu.make_async_copy(
            final.at[:, :, :, at], out.at[:, :, :, at], store_o.at[b]
        )

    c_re, c_im = coefficients(0)
    source_load.wait()
    for b in range(rows):
        at = slice(b * size, (b + 1) * size)
        for k in range(panels):
            re, im = reflected(src[k, 0, :, at], src[k, 1, :, at], c_re[:, at], c_im[:, at])
            field[0, rows + b, k * part:(k + 1) * part] = re
            field[0, rows + b, half + k * part:half + (k + 1) * part] = im
        if b == 0:
            pl.semaphore_wait(barrier, 2 + has_onward.astype(jnp.int32))
        if b < rows // 2:
            across(0, b).start()
    exchange_cols().start()
    for b in range(rows):
        exchange(b).start()

    for b in range(rows):
        split_slot(0, rows + b)
    for b in range(rows):
        weight_loads[b].wait()
        split_row(depth, b)
        if b < rows - rows // 2:
            across(0, b + rows // 2).start()
        if b >= rows // 2:
            pass_on(0, b - rows // 2)
    early = rows // 2
    for b in range(rows - rows // 2, rows):
        pass_on(0, b)
    for b in range(early):
        split_received(b)
    exchange_cols().wait_recv()
    listed = pltpu.make_async_copy(cols_in, cols_other, load_c.at[0])
    listed.start()

    @pl.when(depth == 1)
    def _():
        for b in range(early, rows):
            split_received(b)

    listed.wait()
    finish_halo(0)

    c_re, c_im = coefficients(1)
    for b in range(rows):
        at = slice(b * size, (b + 1) * size)
        re, im = reflected(*row_of(0, b), c_re[:, at], c_im[:, at])
        field[1, rows + b, 0:half] = re
        field[1, rows + b, half:full] = im
        across(1, b).start()
    for b in range(rows):
        split_slot(1, rows + b)

    @pl.when(depth == 0)
    def _():
        for b in range(early, rows):
            split_received(b)

    for b in range(rows):
        pass_on(1, b)
    finish_halo(1)
    for b in range(rows):
        at = slice(b * size, (b + 1) * size)
        re, im = row_of(1, b)
        for k in range(panels):
            final[k, 0, :, at] = re[k * part:(k + 1) * part]
            final[k, 1, :, at] = im[k * part:(k + 1) * part]
        store(b).start()

    exchange_cols().wait_send()
    for b in range(rows):
        exchange(b).wait_send()
        for l in range(2):
            across(l, b).wait_send()

    @pl.when(has_onward)
    def _():
        for l in range(2):
            for b in range(rows):
                along(l, b).wait_send()

    for b in range(rows):
        store(b).wait()


def per_device(sources, blocks, block_cols, refl_level, refl_coef):
    lat_count = lax.axis_size("lat")
    assert lax.axis_size("depth") == 2 and blocks.shape[0] == 1 and lat_count % 2 == 0
    panels, _, part, points = sources.shape
    _, rows, per_row, _, size, _ = blocks.shape
    full = 2 * panels * part
    f32, bf16 = jnp.float32, jnp.bfloat16
    dma = pltpu.SemaphoreType.DMA
    anywhere = pl.BlockSpec(memory_space=pl.ANY)
    flops = 2 * 3 * 2 * full * rows * per_row * size * size * 2
    return pl.pallas_call(
        functools.partial(kernel, lat_count),
        out_shape=jax.ShapeDtypeStruct(sources.shape, f32),
        in_specs=[
            anywhere,
            pl.BlockSpec(memory_space=pltpu.SMEM),
            anywhere,
            anywhere,
            anywhere,
            anywhere,
        ],
        out_specs=anywhere,
        scratch_shapes=[
            pltpu.VMEM((2, rows, per_row, 2, size, size), f32),
            pltpu.VMEM((2, rows, per_row * size, 2 * size), bf16),
            pltpu.VMEM((2, rows, per_row * size, 2 * size), bf16),
            pltpu.VMEM((panels, 2, part, points), f32),
            pltpu.VMEM((1, points), jnp.int32),
            pltpu.VMEM((2, points), f32),
            pltpu.VMEM((2, 3 * rows, full, size), f32),
            pltpu.VMEM((2, 3 * rows, 2 * full, size), bf16),
            pltpu.VMEM((panels, 2, part, points), f32),
            pltpu.VMEM(block_cols.shape, jnp.int32),
            pltpu.SMEM(block_cols.shape, jnp.int32),
            dma((rows,)), dma((1,)), dma((2,)), dma((1,)),
            dma((rows,)), dma((rows,)), dma((1,)), dma((1,)),
            dma((2, rows)), dma((2, rows)), dma((2, rows)), dma((2, rows)), dma((rows,)),
        ],
        compiler_params=pltpu.CompilerParams(
            collective_id=0, has_side_effects=True, vmem_limit_bytes=63 * 1024 * 1024
        ),
        cost_estimate=pl.CostEstimate(
            flops=flops, bytes_accessed=4 * (blocks.size + 2 * sources.size), transcendentals=0
        ),
    )(blocks, block_cols, block_cols, sources, refl_level.reshape(1, points), refl_coef)


def solution(mesh):
    placed = (
        P("shot", None, "depth", "lat"),
        P(("shot", "depth"), "lat", None, None, None, None),
        P("depth", "lat", None),
        P("lat"),
        P(None, "lat"),
    )
    return jax.shard_map(
        per_device,
        mesh=mesh,
        in_specs=placed,
        out_specs=P("shot", None, "depth", "lat"),
        check_vma=False,
    )
```

```python
import functools

import jax
import jax.numpy as jnp
from jax import lax
from jax.experimental import pallas as pl
from jax.experimental.pallas import tpu as pltpu
from jax.sharding import PartitionSpec as P

MESH = pl.DeviceIdType.MESH


def split_bf16(value):
    high = value.astype(jnp.bfloat16)
    low = (value - high.astype(jnp.float32)).astype(jnp.bfloat16)
    return high, low


def kernel(
    lat_count, blocks, cols, cols_hbm, sources, level, coef, out,
    raw, w_hi, w_lo, src, lev, cf, field, parts, final, cols_in, cols_other,
    load_w, load_s, load_r, load_c, send_w, recv_w, send_i, recv_i,
    send_x, recv_x, send_z, recv_z, store_o,
):
    panels, _, part, points = sources.shape
    _, rows, per_row, _, size, _ = blocks.shape
    half = panels * part
    full = 2 * half
    depth = lax.axis_index("depth")
    lat = lax.axis_index("lat")
    odd = lax.rem(lat, 2)
    pair = lat + 1 - 2 * odd
    onward = lat + 2 - 4 * odd
    behind = lat - 2 + 4 * odd
    has_onward = jnp.logical_and(onward >= 0, onward < lat_count)
    has_behind = jnp.logical_and(behind >= 0, behind < lat_count)
    near = 2 * rows * (1 - odd)
    far = 2 * rows * odd

    weight_loads = [
        pltpu.make_async_copy(blocks.at[0, b], raw.at[depth, b], load_w.at[b])
        for b in range(rows)
    ]
    source_load = pltpu.make_async_copy(sources, src, load_s.at[0])
    refl_loads = [
        pltpu.make_async_copy(level, lev, load_r.at[0]),
        pltpu.make_async_copy(coef, cf, load_r.at[1]),
    ]
    for copy in refl_loads + [source_load] + weight_loads:
        copy.start()

    barrier = pltpu.get_barrier_semaphore()
    pl.semaphore_signal(barrier, device_id={"depth": 1 - depth, "lat": lat}, device_id_type=MESH)
    pl.semaphore_signal(barrier, device_id={"depth": depth, "lat": pair}, device_id_type=MESH)

    @pl.when(has_behind)
    def _():
        pl.semaphore_signal(barrier, device_id={"depth": depth, "lat": behind}, device_id_type=MESH)

    for copy in refl_loads:
        copy.wait()

    def coefficients(at):
        here = lev[...] == at
        zero = jnp.float32(0.0)
        return jnp.where(here, cf[0:1, :], zero), jnp.where(here, cf[1:2, :], zero)

    def reflected(re, im, c_re, c_im):
        return re + c_re * re - c_im * im, im + c_re * im + c_im * re

    def send(src_ref, dst_ref, send_sem, recv_sem, to_depth, to_lat):
        return pltpu.make_async_remote_copy(
            src_ref=src_ref, dst_ref=dst_ref, send_sem=send_sem, recv_sem=recv_sem,
            device_id={"depth": to_depth, "lat": to_lat}, device_id_type=MESH,
        )

    def across(l, b):
        return send(
            field.at[l, rows + b], field.at[l, far + b],
            send_x.at[l, b], recv_x.at[l, b], depth, pair,
        )

    def along(l, b):
        return send(
            field.at[l, near + b], field.at[l, far + b],
            send_z.at[l, b], recv_z.at[l, b], depth, onward,
        )

    def exchange(b):
        return send(
            blocks.at[0, b], raw.at[depth, b], send_w.at[b], recv_w.at[b], 1 - depth, lat,
        )

    def exchange_cols():
        return send(cols_hbm, cols_in, send_i.at[0], recv_i.at[0], 1 - depth, lat)

    def split_slot(l, slot):
        high, low = split_bf16(field[l, slot])
        parts[l, slot, 0:full] = high
        parts[l, slot, full:2 * full] = low

    def split_row(l, b):
        for j in range(per_row):
            at = slice(j * size, (j + 1) * size)
            for c in range(2):
                high, low = split_bf16(raw[l, b, j, c])
                w_hi[l, b, at, c * size:(c + 1) * size] = high
                w_lo[l, b, at, c * size:(c + 1) * size] = low

    def split_received(b):
        exchange(b).wait_recv()
        split_row(1 - depth, b)

    def finish_halo(l):
        @pl.when(has_behind)
        def _():
            for b in range(rows):
                along(l, b).wait_recv()
                split_slot(l, far + b)

    def pass_on(l, b):
        across(l, b).wait_recv()

        @pl.when(has_onward)
        def _():
            along(l, b).start()

        split_slot(l, near + b)

    base = (lat - 1) * rows

    def column(l, b, j):
        listed = jnp.where(depth == l, cols[0, b, j], cols_other[0, b, j])
        return jnp.clip(listed - base, 0, 3 * rows - 1)

    def row_of(l, b):
        picked = jnp.concatenate([parts[l, column(l, b, j)] for j in range(per_row)], axis=1)
        both = jnp.dot(picked, w_hi[l, b], preferred_element_type=jnp.float32)
        rest = jnp.dot(picked[:full], w_lo[l, b], preferred_element_type=jnp.float32)
        total = both[:full] + (both[full:] + rest)
        of_re, of_im = total[:half], total[half:]
        return of_re[:, :size] - of_im[:, size:], of_re[:, size:] + of_im[:, :size]

    def store(b):
        at = pl.ds(b * size, size)
        return pltpu.make_async_copy(
            final.at[:, :, :, at], out.at[:, :, :, at], store_o.at[b]
        )

    c_re, c_im = coefficients(0)
    source_load.wait()
    for b in range(rows):
        at = slice(b * size, (b + 1) * size)
        for k in range(panels):
            re, im = reflected(src[k, 0, :, at], src[k, 1, :, at], c_re[:, at], c_im[:, at])
            field[0, rows + b, k * part:(k + 1) * part] = re
            field[0, rows + b, half + k * part:half + (k + 1) * part] = im
        if b == 0:
            pl.semaphore_wait(barrier, 2 + has_onward.astype(jnp.int32))
        if b < rows // 2:
            across(0, b).start()
    exchange_cols().start()
    for b in range(rows):
        exchange(b).start()

    for b in range(rows):
        split_slot(0, rows + b)
    for b in range(rows):
        weight_loads[b].wait()
        split_row(depth, b)
        if b < rows - rows // 2:
            across(0, b + rows // 2).start()
        if b >= rows // 2:
            pass_on(0, b - rows // 2)
    for b in range(rows - rows // 2, rows):
        pass_on(0, b)
    exchange_cols().wait_recv()
    listed = pltpu.make_async_copy(cols_in, cols_other, load_c.at[0])
    listed.start()

    @pl.when(depth == 1)
    def _():
        for b in range(rows):
            split_received(b)

    listed.wait()
    finish_halo(0)

    c_re, c_im = coefficients(1)
    for b in range(rows):
        at = slice(b * size, (b + 1) * size)
        re, im = reflected(*row_of(0, b), c_re[:, at], c_im[:, at])
        field[1, rows + b, 0:half] = re
        field[1, rows + b, half:full] = im
        across(1, b).start()
    for b in range(rows):
        split_slot(1, rows + b)

    @pl.when(depth == 0)
    def _():
        for b in range(rows):
            split_received(b)

    for b in range(rows):
        pass_on(1, b)
    finish_halo(1)
    for b in range(rows):
        at = slice(b * size, (b + 1) * size)
        re, im = row_of(1, b)
        for k in range(panels):
            final[k, 0, :, at] = re[k * part:(k + 1) * part]
            final[k, 1, :, at] = im[k * part:(k + 1) * part]
        store(b).start()

    exchange_cols().wait_send()
    for b in range(rows):
        exchange(b).wait_send()
        for l in range(2):
            across(l, b).wait_send()

    @pl.when(has_onward)
    def _():
        for l in range(2):
            for b in range(rows):
                along(l, b).wait_send()

    for b in range(rows):
        store(b).wait()


def per_device(sources, blocks, block_cols, refl_level, refl_coef):
    lat_count = lax.axis_size("lat")
    assert lax.axis_size("depth") == 2 and blocks.shape[0] == 1 and lat_count % 2 == 0
    panels, _, part, points = sources.shape
    _, rows, per_row, _, size, _ = blocks.shape
    full = 2 * panels * part
    f32, bf16 = jnp.float32, jnp.bfloat16
    dma = pltpu.SemaphoreType.DMA
    anywhere = pl.BlockSpec(memory_space=pl.ANY)
    flops = 2 * 3 * 2 * full * rows * per_row * size * size * 2
    return pl.pallas_call(
        functools.partial(kernel, lat_count),
        out_shape=jax.ShapeDtypeStruct(sources.shape, f32),
        in_specs=[
            anywhere,
            pl.BlockSpec(memory_space=pltpu.SMEM),
            anywhere,
            anywhere,
            anywhere,
            anywhere,
        ],
        out_specs=anywhere,
        scratch_shapes=[
            pltpu.VMEM((2, rows, per_row, 2, size, size), f32),
            pltpu.VMEM((2, rows, per_row * size, 2 * size), bf16),
            pltpu.VMEM((2, rows, per_row * size, 2 * size), bf16),
            pltpu.VMEM((panels, 2, part, points), f32),
            pltpu.VMEM((1, points), jnp.int32),
            pltpu.VMEM((2, points), f32),
            pltpu.VMEM((2, 3 * rows, full, size), f32),
            pltpu.VMEM((2, 3 * rows, 2 * full, size), bf16),
            pltpu.VMEM((panels, 2, part, points), f32),
            pltpu.VMEM(block_cols.shape, jnp.int32),
            pltpu.SMEM(block_cols.shape, jnp.int32),
            dma((rows,)), dma((1,)), dma((2,)), dma((1,)),
            dma((rows,)), dma((rows,)), dma((1,)), dma((1,)),
            dma((2, rows)), dma((2, rows)), dma((2, rows)), dma((2, rows)), dma((rows,)),
        ],
        compiler_params=pltpu.CompilerParams(
            collective_id=0, has_side_effects=True, vmem_limit_bytes=63 * 1024 * 1024
        ),
        cost_estimate=pl.CostEstimate(
            flops=flops, bytes_accessed=4 * (blocks.size + 2 * sources.size), transcendentals=0
        ),
    )(blocks, block_cols, block_cols, sources, refl_level.reshape(1, points), refl_coef)


def solution(mesh):
    placed = (
        P("shot", None, "depth", "lat"),
        P(("shot", "depth"), "lat", None, None, None, None),
        P("depth", "lat", None),
        P("lat"),
        P(None, "lat"),
    )
    return jax.shard_map(
        per_device,
        mesh=mesh,
        in_specs=placed,
        out_specs=P("shot", None, "depth", "lat"),
        check_vma=False,
    )
```
